32 devices in a mesh: gx: 4 (over y, core), gy: 2 (over x), gz: 4 (over z).
Axes of the slice: x: 2, y: 2, z: 4, core: 2. Of those that a mesh axis runs over, the one named last changes fastest.
Arguments:
- stem: bfloat16 [2, 4, 2, 4, 256, 1024], P(None, 'gx', 'gy', 'gz'), may hold values from -6 to 6
- branch_one: bfloat16 [2, 2, 1024, 1024], replicated, may hold values from -0.125 to 0.125
- branch_two: bfloat16 [2, 2, 1024, 1024], P(None, None, ('gy', 'gz')), may hold values from -0.1875 to 0.1875
- branch_three: bfloat16 [2, 2, 1024, 1024], P(None, None, 'gz'), may hold values from -0.125 to 0.125
- slice_values: int32 [3], replicated, may hold values from 0 to 1, as said below
Outputs:
- contracted: bfloat16 [2, 4, 2, 4, 256, 1024], P(None, 'gx', 'gy', 'gz')
The draws below stay inside these ranges and needn't reach their ends.
Inputs may be any that keep to these rules, and one draw needn't show every extreme that they name: `slice_values`: the first two slices differ.
All inputs are finite; a program needn't handle non-finite values.
Results may differ from the reference program's by a relative error of at most 0.0057.
Values may be sent and summed in bfloat16 or wider, within the bound.
A program may use at most 128 MiB of HBM per device.

```python
import jax
import jax.numpy as jnp
from jax import lax

WIDTH = 1024
ROWS = 256
SLICES = 2
N_GX = 4
N_GY = 2
N_GZ = 4


def draw_slice_values(key, part):
    first_key = jax.random.fold_in(key, 11)
    step_key = jax.random.fold_in(key, 12)
    third_key = jax.random.fold_in(key, 13)
    first = jax.random.randint(first_key, (1,), 0, SLICES, dtype=jnp.int32)
    step = jax.random.randint(step_key, (1,), 1, SLICES, dtype=jnp.int32)
    second = (first + step) % SLICES
    third = jax.random.randint(third_key, (1,), 0, SLICES, dtype=jnp.int32)
    return jnp.concatenate([first, second, third]).astype(jnp.int32)


def with_spikes(array, rng, source, target, parts, factor):
    def block_of(dim):
        return (jnp.arange(array.shape[dim]) // (array.shape[dim] // parts)).reshape((-1,) + (1,) * (array.ndim - 1 - dim))

    first = jax.random.permutation(rng, parts)[block_of(target)]
    second = (block_of(target) + parts // 2) % parts
    return jnp.where((block_of(source) == first) | (block_of(source) == second), factor * array, array)


def level_of(stream_key, dims, pieces, low, top_value):
    level, own = 1.0, jax.random.fold_in(stream_key, 6)
    for position, shards_of in pieces:
        steps = jnp.exp(jax.random.uniform(jax.random.fold_in(own, position), (shards_of,), jnp.float32, low / len(pieces), top_value / len(pieces)))
        level = level * jnp.repeat(steps, dims[position] // shards_of).reshape([-1 if axis == position else 1 for axis in range(len(dims))])
    return level


def centred(stream_key, dims, deviation, reach, pieces=(), kind=jnp.bfloat16):
    values = jax.random.normal(stream_key, dims, jnp.float32) * deviation
    if len(pieces) > 0:
        values = level_of(stream_key, dims, pieces, -0.22, 0.18) * values
    return jnp.clip(values, min=-reach, max=reach).astype(kind)


def bell_draw_with(stream_key, extent, width, reach, shards, heavy, kind=jnp.bfloat16):
    values = width * jax.random.normal(stream_key, extent, jnp.float32)
    if shards:
        values = values * level_of(stream_key, extent, shards, -0.22, 0.18)
    return jnp.clip(with_spikes(values, jax.random.fold_in(stream_key, 3), *heavy), -reach, reach).astype(kind)


def setup_inputs(seed: int = 0) -> dict:
    keys = jax.random.split(jax.random.key(seed), 6)
    stem = centred(keys[0], (2, N_GX, N_GY, N_GZ, ROWS, WIDTH), 1.0, 6.0, ((1, 4), (2, 2), (3, 4)))
    branch_one = centred(keys[1], (SLICES, 2, WIDTH, WIDTH), (2 * WIDTH) ** -0.5, 0.125)
    branch_two = bell_draw_with(keys[2], (SLICES, 2, WIDTH, WIDTH), (2 * WIDTH) ** -0.5, 0.1875, ((2, 8),), (2, 3, 8, 2.0))
    branch_three = centred(keys[3], (SLICES, 2, WIDTH, WIDTH), (2 * WIDTH) ** -0.5, 0.125, ((2, 4),))
    slice_values = draw_slice_values(jax.random.fold_in(keys[5], 71), 0)
    return dict(stem=stem, branch_one=branch_one, branch_two=branch_two, branch_three=branch_three, slice_values=slice_values)


def complex_matrix(branch):
    top_half = jnp.concatenate([branch[0], branch[1]], axis=1)
    bottom_half = jnp.concatenate([-branch[1], branch[0]], axis=1)
    return jnp.concatenate([top_half, bottom_half], axis=0)


def complex_product(operand, branch):
    joined = jnp.concatenate([operand[0], operand[1]], axis=1)
    result = jnp.dot(joined, complex_matrix(branch), preferred_element_type=jnp.float32)
    columns = branch.shape[2]
    return jnp.stack([result[:, :columns], result[:, columns:]])


def reference(stem, branch_one, branch_two, branch_three, slice_values):
    group_one = N_GX * N_GY
    group_two = N_GY * N_GZ
    rows_one = ROWS // group_one
    part_one = WIDTH // group_one
    part_two = WIDTH // group_two
    first_branch = lax.dynamic_index_in_dim(branch_one, slice_values[0], 0, keepdims=False)
    second_branch = lax.dynamic_index_in_dim(branch_two, slice_values[1], 0, keepdims=False)
    third_branch = lax.dynamic_index_in_dim(branch_three, slice_values[2], 0, keepdims=False)
    blocks = stem.reshape(2, group_one, N_GZ, N_GX, N_GY, rows_one, part_one, group_one)
    blocks = blocks.transpose(3, 0, 1, 2, 4, 5, 6, 7)

    def one_block(stem_block):
        ordered = stem_block.transpose(0, 3, 2, 4, 6, 1, 5).reshape(2, group_two * ROWS, WIDTH)
        middle = complex_product(ordered, first_branch).astype(jnp.bfloat16)
        middle = middle.reshape(2, group_two, ROWS, part_two, group_two).transpose(0, 2, 4, 1, 3)
        middle = middle.reshape(2, ROWS * group_two, WIDTH)
        second = complex_product(middle, second_branch).astype(jnp.bfloat16)
        second = second.reshape(2, ROWS, group_two, group_two, part_two).transpose(0, 3, 1, 2, 4)
        second = second.reshape(2, group_two * ROWS, WIDTH)
        return complex_product(second, third_branch).astype(jnp.bfloat16)

    mapped = lax.map(one_block, blocks)
    return mapped.transpose(1, 0, 2, 3).reshape(2, N_GX, N_GY, N_GZ, ROWS, WIDTH)
```

```python
import functools

import jax
import jax.numpy as jnp
from jax import lax
from jax.experimental import pallas as pl
from jax.experimental.pallas import tpu as pltpu
from jax.sharding import PartitionSpec as P

WIDTH = 1024
ROWS = 256


def complex_matrix(branch):
    top_half = jnp.concatenate([branch[0], branch[1]], axis=1)
    bottom_half = jnp.concatenate([-branch[1], branch[0]], axis=1)
    return jnp.concatenate([top_half, bottom_half], axis=0)


def complex_product(operand, branch):
    joined = jnp.concatenate([operand[0], operand[1]], axis=1)
    result = jnp.dot(joined, complex_matrix(branch), preferred_element_type=jnp.float32)
    columns = branch.shape[2]
    return jnp.stack([result[:, :columns], result[:, columns:]])


def split_result(result):
    columns = result.shape[1] // 2
    return jnp.stack([result[:, :columns], result[:, columns:]])


def make_accumulate(operand, shard_rows):
    real_part = operand[0]
    imag_part = operand[1]
    joined = jnp.concatenate([real_part, imag_part], axis=1)
    return jnp.dot(joined, complex_matrix(shard_rows), preferred_element_type=jnp.float32)


def third_contraction(operand, branch_three, slice_values):
    local_third = lax.dynamic_index_in_dim(branch_three, slice_values[2], 0, keepdims=False)
    summed = make_accumulate(operand, lax.all_gather(local_third, "gz", axis=1, tiled=True))
    return split_result(summed).astype(jnp.bfloat16)


def body(stem, branch_one, branch_two, branch_three, slice_values):
    count_gx = lax.axis_size("gx")
    count_gy = lax.axis_size("gy")
    count_gz = lax.axis_size("gz")
    group_one = count_gx * count_gy
    group_two = count_gy * count_gz
    rows_one = ROWS // group_one
    rows_two = ROWS // group_two
    part_one = WIDTH // group_one
    part_two = WIDTH // group_two
    first_branch = lax.dynamic_index_in_dim(branch_one, slice_values[0], 0, keepdims=False)
    arrived = lax.all_to_all(
        stem.reshape(2, 1, group_one, rows_one, WIDTH),
        ("gx", "gy"),
        split_axis=2,
        concat_axis=1,
        tiled=True,
    )
    ordered = arrived.reshape(2, group_one, rows_one, part_one, group_one).transpose(0, 2, 4, 1, 3)
    ordered = ordered.reshape(2, ROWS, WIDTH)
    middle = complex_product(ordered, first_branch).astype(jnp.bfloat16)
    gathered = lax.all_to_all(
        middle.reshape(2, group_two, 1, rows_two, WIDTH),
        ("gy", "gz"),
        split_axis=1,
        concat_axis=2,
        tiled=True,
    )
    regrouped = gathered.reshape(2, group_two, rows_two, part_two, group_two).transpose(
        0, 2, 4, 1, 3
    )
    regrouped = regrouped.reshape(2, ROWS, WIDTH)
    local_second = lax.dynamic_index_in_dim(branch_two, slice_values[1], 0, keepdims=False)
    summed = make_accumulate(
        regrouped, lax.all_gather(local_second, ("gy", "gz"), axis=1, tiled=True)
    )
    second = split_result(summed).astype(jnp.bfloat16)
    returned = lax.all_to_all(
        second.reshape(2, 1, rows_two, group_two, group_two, part_two),
        ("gy", "gz"),
        split_axis=4,
        concat_axis=1,
        tiled=True,
    )
    result = third_contraction(returned.reshape(2, ROWS, WIDTH), branch_three, slice_values)
    return result.reshape(stem.shape)


MESH = pl.DeviceIdType.MESH
VMEM_LIMIT = 56 * 1024 * 1024
TILE = 256
LANE = 128


def complex_tile(lhs, rhs):
    result = jnp.dot(lhs, rhs, preferred_element_type=jnp.float32)
    m, n = result.shape[0] // 2, result.shape[1] // 2
    real = result[:m, :n] - result[m:, n:]
    imag = result[m:, :n] + result[:m, n:]
    return real.astype(jnp.bfloat16), imag.astype(jnp.bfloat16)


def kernel(
    dims, slices, stem, one_hbm, two_in, three_in, out,
    perm, one, one_perm, two, three, sorted_stem, first, second, third, result,
    one_sem, own_sem, stem_send, stem_recv, part_send, part_recv, back_send, back_recv,
):
    nx, ny, nz = dims
    group = ny * nz
    devices = nx * group
    gx, gy, gz = lax.axis_index("gx"), lax.axis_index("gy"), lax.axis_index("gz")
    line, core = gx // 2, gx % 2
    me = (gx * ny + gy) * nz + gz
    place = gy * nz + gz

    load_one = pltpu.make_async_copy(one_hbm, one, one_sem)
    load_one.start()

    def coordinates(index):
        return (index // group, (index // nz) % ny, index % nz)

    barrier = pltpu.get_barrier_semaphore()

    def greet(step, carry):
        pl.semaphore_signal(
            barrier, inc=1, device_id=coordinates((me + step) % devices), device_id_type=MESH
        )
        return carry

    lax.fori_loop(1, devices, greet, 0)

    rows_two, rows_three = WIDTH // group, WIDTH // nz
    piece = rows_two // nx
    two[:, pl.ds(pl.multiple_of(place * rows_two, rows_two), rows_two), :] = two_in[slices[1]]
    three[:, pl.ds(pl.multiple_of(gz * rows_three, rows_three), rows_three), :] = three_in[slices[2]]

    def make_perm(tile, carry):
        column = lax.broadcasted_iota(jnp.int32, (WIDTH, TILE), 1) + tile * TILE
        row = lax.broadcasted_iota(jnp.int32, (WIDTH, TILE), 0)
        wanted = (column % LANE) * group + column // LANE
        perm[tile] = jnp.where(row == wanted, 1.0, 0.0).astype(jnp.bfloat16)
        return carry

    lax.fori_loop(0, WIDTH // TILE, make_perm, 0)
    pl.semaphore_wait(barrier, devices - 1)

    sends = []

    def piece_two_of(line_of, x, back):
        start = (x * nz + (gz + nz - back) % nz) * rows_two + (line_of * 2 + core) * piece
        return two.at[:, pl.ds(pl.multiple_of(start, piece), piece), :]

    def piece_three_of(line_of, x, back):
        start = ((gz + nz - back) % nz) * rows_three + ((line_of * 2 + core) * ny + x) * piece
        return three.at[:, pl.ds(pl.multiple_of(start, piece), piece), :]

    def send(ref, device):
        index = len(sends)
        copy = pltpu.make_async_remote_copy(
            src_ref=ref, dst_ref=ref,
            send_sem=part_send.at[index], recv_sem=part_recv.at[index],
            device_id=device, device_id_type=MESH,
        )
        copy.start()
        sends.append(copy)
        return copy

    other_line, other_x = 1 - line, 1 - gy
    to_line = (other_line * 2 + core, gy, gz)
    to_x = (gx, other_x, gz)
    to_core = (line * 2 + 1 - core, gy, gz)

    two_z, three_z = {}, {}
    for step in range(1, nz):
        device = (gx, gy, (gz + step) % nz)
        two_z[step] = send(piece_two_of(line, gy, 0), device)
        three_z[step] = send(piece_three_of(line, gy, 0), device)
    two_x = {0: send(piece_two_of(line, gy, 0), to_x)}

    def sort_stem(tile, carry):
        operand = stem[...].reshape(2 * ROWS, WIDTH)
        moved = jnp.dot(operand, perm[tile], preferred_element_type=jnp.float32)
        moved = moved.astype(jnp.bfloat16).reshape(2, ROWS, TILE)
        sorted_stem[:, :, pl.ds(pl.multiple_of(tile * TILE, TILE), TILE)] = moved
        return carry

    lax.fori_loop(0, WIDTH // TILE, sort_stem, 0)
    rows_one = ROWS // nx

    def stem_block(index):
        return sorted_stem.at[
            :,
            pl.ds(pl.multiple_of((index // group) * rows_one, rows_one), rows_one),
            pl.ds(pl.multiple_of((index % group) * LANE, LANE), LANE),
        ]

    def landing(index):
        return first.at[:, index % nz, :, pl.ds(pl.multiple_of((index // nz) * LANE, LANE), LANE)]

    def stem_copy(step):
        target = (me + step) % devices
        return pltpu.make_async_remote_copy(
            src_ref=stem_block(target), dst_ref=landing(me),
            send_sem=stem_send.at[step], recv_sem=stem_recv.at[step],
            device_id=coordinates(target), device_id_type=MESH,
        )

    def send_stem(step, carry):
        stem_copy(step).start()
        return carry

    lax.fori_loop(1, devices, send_stem, 0)
    own = pltpu.make_async_copy(stem_block(me), landing(me), own_sem.at[0])
    own.start()

    load_one.wait()

    def sort_one(tile, carry):
        for part in range(2):
            moved = jnp.dot(
                one[slices[0], part], perm[tile], preferred_element_type=jnp.float32
            ).astype(jnp.bfloat16)
            for half in range(2):
                one_perm[2 * tile + half, :, part * LANE : (part + 1) * LANE] = moved[
                    :, half * LANE : (half + 1) * LANE
                ]
        return carry

    lax.fori_loop(0, WIDTH // TILE, sort_one, 0)

    two_y, three_y, three_x = {}, {}, {}
    two_core, three_core = [], []
    for step in range(1, nz):
        two_z[step].wait_recv()
        two_x[step] = send(piece_two_of(line, gy, step), to_x)
        three_z[step].wait_recv()
        three_y[step] = send(piece_three_of(line, gy, step), to_line)
    for step in range(1, nz):
        two_y[0, step] = send(piece_two_of(line, gy, step), to_line)
        three_x[0, step] = send(piece_three_of(line, gy, step), to_x)
        two_core.append(send(piece_two_of(line, gy, step), to_core))
        three_core.append(send(piece_three_of(line, gy, step), to_core))
    for step in range(nz):
        two_x[step].wait_recv()
        two_y[1, step] = send(piece_two_of(line, other_x, step), to_line)
        two_core.append(send(piece_two_of(line, other_x, step), to_core))
        if step > 0:
            three_y[step].wait_recv()
            three_x[1, step] = send(piece_three_of(other_line, gy, step), to_x)
            three_core.append(send(piece_three_of(other_line, gy, step), to_core))

    own.wait()

    def await_stem(step, carry):
        stem_copy(step).wait_recv()
        return carry

    lax.fori_loop(1, devices, await_stem, 0)
    chunk = ROWS // group

    def contract_first(k, carry):
        operand = first[...].reshape(2 * ROWS, WIDTH)
        for part, value in enumerate(complex_tile(operand, one_perm[k])):
            for c in range(nz):
                for ry in range(ny):
                    row, column = (c * ny + ry) * chunk, (ry * nz + c) * LANE
                    second[part, k, :, column : column + LANE] = value[row : row + chunk]
        return carry

    lax.fori_loop(0, group, contract_first, 0)

    for step in range(1, nz):
        two_y[0, step].wait_recv()
        two_core.append(send(piece_two_of(other_line, gy, step), to_core))
        three_x[0, step].wait_recv()
        three_core.append(send(piece_three_of(line, other_x, step), to_core))
    for step in range(nz):
        two_y[1, step].wait_recv()
        two_core.append(send(piece_two_of(other_line, other_x, step), to_core))
        if step > 0:
            three_x[1, step].wait_recv()
            three_core.append(send(piece_three_of(other_line, other_x, step), to_core))

    for copy in two_core:
        copy.wait_recv()

    def contract_second(s, carry):
        operand = second[...].reshape(2 * ROWS, WIDTH)
        columns = pl.ds(pl.multiple_of(s * LANE, LANE), LANE)
        branch = jnp.concatenate([two[0, :, columns], two[1, :, columns]], axis=1)
        for part, value in enumerate(complex_tile(operand, branch)):
            for k in range(group):
                third[part, s, :, k * LANE : (k + 1) * LANE] = value[k * chunk : (k + 1) * chunk]
        return carry

    lax.fori_loop(0, group, contract_second, 0)

    for copy in three_core:
        copy.wait_recv()
    tiles = WIDTH // TILE

    def back_copy(tile, step):
        target = (place + step) % group
        columns = pl.ds(pl.multiple_of(tile * TILE, TILE), TILE)
        return pltpu.make_async_remote_copy(
            src_ref=result.at[target, :, :, columns], dst_ref=out.at[place, :, :, columns],
            send_sem=back_send.at[tile, step], recv_sem=back_recv.at[tile, step],
            device_id=(gx, target // nz, target % nz), device_id_type=MESH,
        )

    def contract_third(tile, carry):
        operand = third[...].reshape(2 * ROWS, WIDTH)
        columns = pl.ds(pl.multiple_of(tile * TILE, TILE), TILE)
        branch = jnp.concatenate([three[0, :, columns], three[1, :, columns]], axis=1)
        for part, value in enumerate(complex_tile(operand, branch)):
            result[:, part, :, columns] = value.reshape(group, chunk, TILE)

        def send_back(step, inner):
            back_copy(tile, step).start()
            return inner

        lax.fori_loop(1, group, send_back, 0)
        return carry

    lax.fori_loop(0, tiles, contract_third, 0)
    keep = pltpu.make_async_copy(result.at[place], out.at[place], own_sem.at[1])
    keep.start()
    keep.wait()

    for copy in sends:
        copy.wait_send()

    def end_stem(step, carry):
        stem_copy(step).wait_send()
        return carry

    lax.fori_loop(1, devices, end_stem, 0)

    def end_back(index, carry):
        copy = back_copy(index // (group - 1), index % (group - 1) + 1)
        copy.wait_send()
        copy.wait_recv()
        return carry

    lax.fori_loop(0, tiles * (group - 1), end_back, 0)


def fused_body(dims, stem, branch_one, branch_two, branch_three, slice_values):
    nx, ny, nz = dims
    group = ny * nz
    devices = nx * group
    chunk = ROWS // group
    pieces = 2 * (nz - 1) + nz + (nz - 1) + (2 * nz - 1) + 2 * (nz - 1)
    pieces = pieces + 2 * (2 * nz - 1) + 4 * (nz - 1)
    bf16 = jnp.bfloat16
    vmem = pl.BlockSpec(memory_space=pltpu.VMEM)
    dma = pltpu.SemaphoreType.DMA
    blocks = pl.pallas_call(
        functools.partial(kernel, dims),
        out_shape=jax.ShapeDtypeStruct((group, 2, chunk, WIDTH), bf16),
        in_specs=[
            pl.BlockSpec(memory_space=pltpu.SMEM),
            vmem,
            pl.BlockSpec(memory_space=pl.ANY),
            vmem,
            vmem,
        ],
        out_specs=pl.BlockSpec(memory_space=pl.ANY),
        scratch_shapes=[
            pltpu.VMEM((WIDTH // TILE, WIDTH, TILE), bf16),
            pltpu.VMEM(branch_one.shape, bf16),
            pltpu.VMEM((group, WIDTH, 2 * LANE), bf16),
            pltpu.VMEM((2, WIDTH, WIDTH), bf16),
            pltpu.VMEM((2, WIDTH, WIDTH), bf16),
            pltpu.VMEM((2, ROWS, WIDTH), bf16),
            pltpu.VMEM((2, nz, ROWS // nx, WIDTH), bf16),
            pltpu.VMEM((2, group, chunk, WIDTH), bf16),
            pltpu.VMEM((2, group, chunk, WIDTH), bf16),
            pltpu.VMEM((group, 2, chunk, WIDTH), bf16),
            dma,
            dma((2,)),
            dma((devices,)),
            dma((devices,)),
            dma((pieces,)),
            dma((pieces,)),
            dma((WIDTH // TILE, group)),
            dma((WIDTH // TILE, group)),
        ],
        compiler_params=pltpu.CompilerParams(
            collective_id=0, has_side_effects=True, vmem_limit_bytes=VMEM_LIMIT
        ),
        cost_estimate=pl.CostEstimate(
            flops=24 * ROWS * WIDTH * WIDTH, bytes_accessed=16 * WIDTH * WIDTH, transcendentals=0
        ),
    )(slice_values, stem.reshape(2, ROWS, WIDTH), branch_one, branch_two, branch_three)
    return blocks.transpose(1, 2, 0, 3).reshape(stem.shape)


def solution(mesh):
    dims = (mesh.shape["gx"], mesh.shape["gy"], mesh.shape["gz"])
    group_one, group_two = dims[0] * dims[1], dims[1] * dims[2]
    fused = group_one == group_two == WIDTH // LANE and dims[0] == 4 and dims[1] == 2
    return jax.shard_map(
        functools.partial(fused_body, dims) if fused else body,
        mesh=mesh,
        in_specs=(
            P(None, "gx", "gy", "gz", None, None),
            P(),
            P(None, None, ("gy", "gz"), None),
            P(None, None, "gz", None),
            P(),
        ),
        out_specs=P(None, "gx", "gy", "gz", None, None),
        check_vma=False,
    )
```

```python
import functools

import jax
import jax.numpy as jnp
from jax import lax
from jax.experimental import pallas as pl
from jax.experimental.pallas import tpu as pltpu
from jax.sharding import PartitionSpec as P

WIDTH = 1024
ROWS = 256


def complex_matrix(branch):
    top_half = jnp.concatenate([branch[0], branch[1]], axis=1)
    bottom_half = jnp.concatenate([-branch[1], branch[0]], axis=1)
    return jnp.concatenate([top_half, bottom_half], axis=0)


def complex_product(operand, branch):
    joined = jnp.concatenate([operand[0], operand[1]], axis=1)
    result = jnp.dot(joined, complex_matrix(branch), preferred_element_type=jnp.float32)
    columns = branch.shape[2]
    return jnp.stack([result[:, :columns], result[:, columns:]])


def split_result(result):
    columns = result.shape[1] // 2
    return jnp.stack([result[:, :columns], result[:, columns:]])


def make_accumulate(operand, shard_rows):
    real_part = operand[0]
    imag_part = operand[1]
    joined = jnp.concatenate([real_part, imag_part], axis=1)
    return jnp.dot(joined, complex_matrix(shard_rows), preferred_element_type=jnp.float32)


def third_contraction(operand, branch_three, slice_values):
    local_third = lax.dynamic_index_in_dim(branch_three, slice_values[2], 0, keepdims=False)
    summed = make_accumulate(operand, lax.all_gather(local_third, "gz", axis=1, tiled=True))
    return split_result(summed).astype(jnp.bfloat16)


def body(stem, branch_one, branch_two, branch_three, slice_values):
    count_gx = lax.axis_size("gx")
    count_gy = lax.axis_size("gy")
    count_gz = lax.axis_size("gz")
    group_one = count_gx * count_gy
    group_two = count_gy * count_gz
    rows_one = ROWS // group_one
    rows_two = ROWS // group_two
    part_one = WIDTH // group_one
    part_two = WIDTH // group_two
    first_branch = lax.dynamic_index_in_dim(branch_one, slice_values[0], 0, keepdims=False)
    arrived = lax.all_to_all(
        stem.reshape(2, 1, group_one, rows_one, WIDTH),
        ("gx", "gy"),
        split_axis=2,
        concat_axis=1,
        tiled=True,
    )
    ordered = arrived.reshape(2, group_one, rows_one, part_one, group_one).transpose(0, 2, 4, 1, 3)
    ordered = ordered.reshape(2, ROWS, WIDTH)
    middle = complex_product(ordered, first_branch).astype(jnp.bfloat16)
    gathered = lax.all_to_all(
        middle.reshape(2, group_two, 1, rows_two, WIDTH),
        ("gy", "gz"),
        split_axis=1,
        concat_axis=2,
        tiled=True,
    )
    regrouped = gathered.reshape(2, group_two, rows_two, part_two, group_two).transpose(
        0, 2, 4, 1, 3
    )
    regrouped = regrouped.reshape(2, ROWS, WIDTH)
    local_second = lax.dynamic_index_in_dim(branch_two, slice_values[1], 0, keepdims=False)
    summed = make_accumulate(
        regrouped, lax.all_gather(local_second, ("gy", "gz"), axis=1, tiled=True)
    )
    second = split_result(summed).astype(jnp.bfloat16)
    returned = lax.all_to_all(
        second.reshape(2, 1, rows_two, group_two, group_two, part_two),
        ("gy", "gz"),
        split_axis=4,
        concat_axis=1,
        tiled=True,
    )
    result = third_contraction(returned.reshape(2, ROWS, WIDTH), branch_three, slice_values)
    return result.reshape(stem.shape)


MESH = pl.DeviceIdType.MESH
VMEM_LIMIT = 56 * 1024 * 1024
TILE = 256
LANE = 128


def complex_tile(lhs, rhs):
    result = jnp.dot(lhs, rhs, preferred_element_type=jnp.float32)
    m, n = result.shape[0] // 2, result.shape[1] // 2
    real = result[:m, :n] - result[m:, n:]
    imag = result[m:, :n] + result[:m, n:]
    return real.astype(jnp.bfloat16), imag.astype(jnp.bfloat16)


def kernel(
    dims, slices, stem, one_hbm, two_in, three_in, out,
    perm, one, one_perm, two, three, sorted_stem, first, second, third, result,
    one_sem, own_sem, stem_send, stem_recv, part_send, part_recv, z_send, z_recv, back_send, back_recv,
):
    nx, ny, nz = dims
    group = ny * nz
    devices = nx * group
    gx, gy, gz = lax.axis_index("gx"), lax.axis_index("gy"), lax.axis_index("gz")
    line, core = gx // 2, gx % 2
    me = (gx * ny + gy) * nz + gz
    place = gy * nz + gz

    load_one = pltpu.make_async_copy(one_hbm, one, one_sem)
    load_one.start()

    def coordinates(index):
        return (index // group, (index // nz) % ny, index % nz)

    barrier = pltpu.get_barrier_semaphore()

    def greet(step, carry):
        pl.semaphore_signal(
            barrier, inc=1, device_id=coordinates((me + step) % devices), device_id_type=MESH
        )
        return carry

    lax.fori_loop(1, devices, greet, 0)

    rows_two, rows_three = WIDTH // group, WIDTH // nz
    piece = rows_two // nx
    two[:, pl.ds(pl.multiple_of(place * rows_two, rows_two), rows_two), :] = two_in[slices[1]]
    three[:, pl.ds(pl.multiple_of(gz * rows_three, rows_three), rows_three), :] = three_in[slices[2]]

    def make_perm(tile, carry):
        column = lax.broadcasted_iota(jnp.int32, (WIDTH, TILE), 1) + tile * TILE
        row = lax.broadcasted_iota(jnp.int32, (WIDTH, TILE), 0)
        wanted = (column % LANE) * group + column // LANE
        perm[tile] = jnp.where(row == wanted, 1.0, 0.0).astype(jnp.bfloat16)
        return carry

    lax.fori_loop(0, WIDTH // TILE, make_perm, 0)
    pl.semaphore_wait(barrier, devices - 1)

    sends = []

    upper = gz // 2
    depth = gz + upper * (nz - 1 - 2 * gz)

    def mirrored(position):
        return position + upper * (nz - 1 - 2 * position)

    def z_of(back):
        return gz if back == 0 else mirrored(1 - depth if back == 1 else back)

    def piece_two_of(line_of, x, back):
        start = (x * nz + z_of(back)) * rows_two + (line_of * 2 + core) * piece
        return two.at[:, pl.ds(pl.multiple_of(start, piece), piece), :]

    def piece_three_of(line_of, x, back):
        start = z_of(back) * rows_three + ((line_of * 2 + core) * ny + x) * piece
        return three.at[:, pl.ds(pl.multiple_of(start, piece), piece), :]

    def send(ref, device):
        index = len(sends)
        copy = pltpu.make_async_remote_copy(
            src_ref=ref, dst_ref=ref,
            send_sem=part_send.at[index], recv_sem=part_recv.at[index],
            device_id=device, device_id_type=MESH,
        )
        copy.start()
        sends.append(copy)
        return copy

    other_line, other_x = 1 - line, 1 - gy
    to_line = (other_line * 2 + core, gy, gz)
    to_x = (gx, other_x, gz)
    to_core = (line * 2 + 1 - core, gy, gz)

    pieces_of = (piece_two_of, piece_three_of)

    def z_copy(kind, back, hop, position):
        ref = pieces_of[kind](line, gy, back)
        return pltpu.make_async_remote_copy(
            src_ref=ref, dst_ref=ref,
            send_sem=z_send.at[kind, hop], recv_sem=z_recv.at[kind, z_of(back)],
            device_id=(gx, gy, mirrored(position)), device_id_type=MESH,
        )

    def z_hops(back):
        return [z_copy(kind, back, 1 + back, 2 if back < 2 else 0) for kind in range(2)]

    for kind in range(2):
        z_copy(kind, 0, 0, 1 - depth).start()

    @pl.when(depth == 1)
    def _():
        for copy in z_hops(0):
            copy.start()

    def pass_on(back):
        for kind in range(2):
            z_copy(kind, back, 0, 0).wait_recv()

        @pl.when(depth == 1)
        def _():
            for copy in z_hops(back):
                copy.start()

    two_y, three_y, three_x = {}, {}, {}
    two_core, three_core = [], []
    two_x = {0: send(piece_two_of(line, gy, 0), to_x)}

    def sort_stem(tile, carry):
        operand = stem[...].reshape(2 * ROWS, WIDTH)
        moved = jnp.dot(operand, perm[tile], preferred_element_type=jnp.float32)
        moved = moved.astype(jnp.bfloat16).reshape(2, ROWS, TILE)
        sorted_stem[:, :, pl.ds(pl.multiple_of(tile * TILE, TILE), TILE)] = moved
        return carry

    lax.fori_loop(0, WIDTH // TILE, sort_stem, 0)
    rows_one = ROWS // nx

    def stem_block(index):
        return sorted_stem.at[
            :,
            pl.ds(pl.multiple_of((index // group) * rows_one, rows_one), rows_one),
            pl.ds(pl.multiple_of((index % group) * LANE, LANE), LANE),
        ]

    def landing(index):
        return first.at[:, index % nz, :, pl.ds(pl.multiple_of((index // nz) * LANE, LANE), LANE)]

    def stem_copy(step):
        target = (me + step) % devices
        return pltpu.make_async_remote_copy(
            src_ref=stem_block(target), dst_ref=landing(me),
            send_sem=stem_send.at[step], recv_sem=stem_recv.at[step],
            device_id=coordinates(target), device_id_type=MESH,
        )

    def send_plane(step, carry):
        stem_copy(step * nz).start()
        return carry

    def send_stem_rest(step, carry):
        stem_copy(step + step // (nz - 1) + 1).start()
        return carry

    lax.fori_loop(1, devices // nz, send_plane, 0)
    own = pltpu.make_async_copy(stem_block(me), landing(me), own_sem.at[0])
    own.start()

    for step in range(1, nz):
        pass_on(step)
        two_x[step] = send(piece_two_of(line, gy, step), to_x)
        three_y[step] = send(piece_three_of(line, gy, step), to_line)
    for step in range(1, nz):
        two_y[0, step] = send(piece_two_of(line, gy, step), to_line)
        three_x[0, step] = send(piece_three_of(line, gy, step), to_x)
    lax.fori_loop(0, devices - devices // nz, send_stem_rest, 0)
    for step in range(1, nz):
        two_core.append(send(piece_two_of(line, gy, step), to_core))
        three_core.append(send(piece_three_of(line, gy, step), to_core))

    load_one.wait()

    def sort_one(tile, carry):
        for part in range(2):
            moved = jnp.dot(
                one[slices[0], part], perm[tile], preferred_element_type=jnp.float32
            ).astype(jnp.bfloat16)
            for half in range(2):
                one_perm[2 * tile + half, :, part * LANE : (part + 1) * LANE] = moved[
                    :, half * LANE : (half + 1) * LANE
                ]
        return carry

    lax.fori_loop(0, WIDTH // TILE, sort_one, 0)

    for step in range(nz):
        two_x[step].wait_recv()
        two_y[1, step] = send(piece_two_of(line, other_x, step), to_line)
        two_core.append(send(piece_two_of(line, other_x, step), to_core))
        if step > 0:
            three_y[step].wait_recv()
            three_x[1, step] = send(piece_three_of(other_line, gy, step), to_x)
            three_core.append(send(piece_three_of(other_line, gy, step), to_core))

    own.wait()

    def await_stem(step, carry):
        stem_copy(step).wait_recv()
        return carry

    lax.fori_loop(1, devices, await_stem, 0)
    chunk = ROWS // group

    def contract_first(k, carry):
        operand = first[...].reshape(2 * ROWS, WIDTH)
        for part, value in enumerate(complex_tile(operand, one_perm[k])):
            for c in range(nz):
                for ry in range(ny):
                    row, column = (c * ny + ry) * chunk, (ry * nz + c) * LANE
                    second[part, k, :, column : column + LANE] = value[row : row + chunk]
        return carry

    lax.fori_loop(0, group, contract_first, 0)

    for step in range(1, nz):
        two_y[0, step].wait_recv()
        two_core.append(send(piece_two_of(other_line, gy, step), to_core))
        three_x[0, step].wait_recv()
        three_core.append(send(piece_three_of(line, other_x, step), to_core))
    for step in range(nz):
        two_y[1, step].wait_recv()
        two_core.append(send(piece_two_of(other_line, other_x, step), to_core))
        if step > 0:
            three_x[1, step].wait_recv()
            three_core.append(send(piece_three_of(other_line, other_x, step), to_core))

    for copy in two_core:
        copy.wait_recv()

    def contract_second(s, carry):
        operand = second[...].reshape(2 * ROWS, WIDTH)
        columns = pl.ds(pl.multiple_of(s * LANE, LANE), LANE)
        branch = jnp.concatenate([two[0, :, columns], two[1, :, columns]], axis=1)
        for part, value in enumerate(complex_tile(operand, branch)):
            for k in range(group):
                third[part, s, :, k * LANE : (k + 1) * LANE] = value[k * chunk : (k + 1) * chunk]
        return carry

    lax.fori_loop(0, group, contract_second, 0)

    for copy in three_core:
        copy.wait_recv()
    tiles = WIDTH // TILE

    def back_copy(tile, step):
        target = (place + step) % group
        columns = pl.ds(pl.multiple_of(tile * TILE, TILE), TILE)
        return pltpu.make_async_remote_copy(
            src_ref=result.at[target, :, :, columns], dst_ref=out.at[place, :, :, columns],
            send_sem=back_send.at[tile, step], recv_sem=back_recv.at[tile, step],
            device_id=(gx, target // nz, target % nz), device_id_type=MESH,
        )

    def contract_third(tile, carry):
        operand = third[...].reshape(2 * ROWS, WIDTH)
        columns = pl.ds(pl.multiple_of(tile * TILE, TILE), TILE)
        branch = jnp.concatenate([three[0, :, columns], three[1, :, columns]], axis=1)
        for part, value in enumerate(complex_tile(operand, branch)):
            result[:, part, :, columns] = value.reshape(group, chunk, TILE)

        def send_back(step, inner):
            back_copy(tile, step).start()
            return inner

        lax.fori_loop(1, group, send_back, 0)
        return carry

    lax.fori_loop(0, tiles, contract_third, 0)
    keep = pltpu.make_async_copy(result.at[place], out.at[place], own_sem.at[1])
    keep.start()
    keep.wait()

    for copy in sends:
        copy.wait_send()
    for kind in range(2):
        z_copy(kind, 0, 0, 1 - depth).wait_send()

    @pl.when(depth == 1)
    def _():
        for back in range(nz):
            for copy in z_hops(back):
                copy.wait_send()

    def end_stem(step, carry):
        stem_copy(step).wait_send()
        return carry

    lax.fori_loop(1, devices, end_stem, 0)

    def end_back(index, carry):
        copy = back_copy(index // (group - 1), index % (group - 1) + 1)
        copy.wait_send()
        copy.wait_recv()
        return carry

    lax.fori_loop(0, tiles * (group - 1), end_back, 0)


def fused_body(dims, stem, branch_one, branch_two, branch_three, slice_values):
    nx, ny, nz = dims
    group = ny * nz
    devices = nx * group
    chunk = ROWS // group
    pieces = nz + (nz - 1) + (2 * nz - 1) + 2 * (nz - 1)
    pieces = pieces + 2 * (2 * nz - 1) + 4 * (nz - 1)
    bf16 = jnp.bfloat16
    vmem = pl.BlockSpec(memory_space=pltpu.VMEM)
    dma = pltpu.SemaphoreType.DMA
    blocks = pl.pallas_call(
        functools.partial(kernel, dims),
        out_shape=jax.ShapeDtypeStruct((group, 2, chunk, WIDTH), bf16),
        in_specs=[
            pl.BlockSpec(memory_space=pltpu.SMEM),
            vmem,
            pl.BlockSpec(memory_space=pl.ANY),
            vmem,
            vmem,
        ],
        out_specs=pl.BlockSpec(memory_space=pl.ANY),
        scratch_shapes=[
            pltpu.VMEM((WIDTH // TILE, WIDTH, TILE), bf16),
            pltpu.VMEM(branch_one.shape, bf16),
            pltpu.VMEM((group, WIDTH, 2 * LANE), bf16),
            pltpu.VMEM((2, WIDTH, WIDTH), bf16),
            pltpu.VMEM((2, WIDTH, WIDTH), bf16),
            pltpu.VMEM((2, ROWS, WIDTH), bf16),
            pltpu.VMEM((2, nz, ROWS // nx, WIDTH), bf16),
            pltpu.VMEM((2, group, chunk, WIDTH), bf16),
            pltpu.VMEM((2, group, chunk, WIDTH), bf16),
            pltpu.VMEM((group, 2, chunk, WIDTH), bf16),
            dma,
            dma((2,)),
            dma((devices,)),
            dma((devices,)),
            dma((pieces,)),
            dma((pieces,)),
            dma((2, nz + 1)),
            dma((2, nz)),
            dma((WIDTH // TILE, group)),
            dma((WIDTH // TILE, group)),
        ],
        compiler_params=pltpu.CompilerParams(
            collective_id=0, has_side_effects=True, vmem_limit_bytes=VMEM_LIMIT
        ),
        cost_estimate=pl.CostEstimate(
            flops=24 * ROWS * WIDTH * WIDTH, bytes_accessed=16 * WIDTH * WIDTH, transcendentals=0
        ),
    )(slice_values, stem.reshape(2, ROWS, WIDTH), branch_one, branch_two, branch_three)
    return blocks.transpose(1, 2, 0, 3).reshape(stem.shape)


def solution(mesh):
    dims = (mesh.shape["gx"], mesh.shape["gy"], mesh.shape["gz"])
    group_one, group_two = dims[0] * dims[1], dims[1] * dims[2]
    fused = group_one == group_two == WIDTH // LANE and dims == (4, 2, 4)
    return jax.shard_map(
        functools.partial(fused_body, dims) if fused else body,
        mesh=mesh,
        in_specs=(
            P(None, "gx", "gy", "gz", None, None),
            P(),
            P(None, None, ("gy", "gz"), None),
            P(None, None, "gz", None),
            P(),
        ),
        out_specs=P(None, "gx", "gy", "gz", None, None),
        check_vma=False,
    )
```
